512 devices in a mesh: kring: 32 (over y, z_hi, core), kblk: 16 (over z_lo, x).
Axes of the slice: x: 4, y: 8, z: 8 (z_hi: 2, z_lo: 4; z = z_hi * 4 + z_lo), core: 2. Of those that a mesh axis runs over, the one named last changes fastest.
Arguments:
- elem_x: bfloat16 [32, 16, 128, 1024], P('kring', 'kblk'), may hold values from -6 to 6
- elem_d: bfloat16 [32, 16, 128, 512], P('kring', 'kblk'), may hold values from -6 to 6
- rows_x: bfloat16 [32, 16, 128, 1024], P('kring', 'kblk'), may hold values from -0.1875 to 0.1875
- rows_d: bfloat16 [32, 16, 128, 512], P('kring', 'kblk'), may hold values from -0.25 to 0.25
- coulomb: float32 [1024], replicated, may hold values from 0.2 to 2
- screened: float32 [512], replicated, may hold values from 0.1 to 1
- cutoff: int32 [32, 16, 32], P('kring', 'kblk'), may hold values from 256 to 1024
- owners: int32 [32, 16, 32, 1], P('kring', 'kblk'), may hold values from 0 to 15; in each aligned block of 32 rows (0 to 31, 32 to 63, ..., all dimensions but the last counted through in order) at most 4 rows name the same one
Outputs:
- assembled: bfloat16 [32, 16, 16, 4, 128, 128], P('kring', 'kblk')
The draws below stay inside these ranges and needn't reach their ends.
Inputs may be any that keep to these rules, and one draw needn't show every extreme that they name: `owners`: among the 32 entries of one (i, j), no owner appears more than 4 times, and some owner appears exactly 4 times.
All inputs are finite; a program needn't handle non-finite values.
Results may differ from the reference program's by a relative error of at most 0.0049.
Values may be sent and summed in bfloat16 or wider, within the bound.
No kernel may reach another device: no remote copies, remote signals or barrier semaphores. Data moves between devices by JAX's collectives and lax.ppermute only.
A program may use at most 64 MiB of HBM per device.

```python
import math
import jax
import jax.numpy as jnp
import numpy as np
from jax import lax

TILE = 128
NG = 1024
NGW = 512
CAP = 4
N_KRING = 32
N_KBLK = 16


def plant(values, stream_key, least, high):
    extent = values.shape
    index_at = [jax.random.randint(jax.random.fold_in(stream_key, axis), (), 0, extent[axis]) for axis in range(len(extent))]
    values = values.at[tuple(index_at)].set(least)
    longest = extent.index(max(extent))
    index_at[longest] = (index_at[longest] + 1) % extent[longest]
    return values.at[tuple(index_at)].set(high)


def shard_levels(rng, shape, cuts, smallest, high):
    loudness, own = 1.0, jax.random.fold_in(rng, 6)
    for dim, blocks in cuts:
        draws = jnp.exp(jax.random.uniform(jax.random.fold_in(own, dim), (blocks,), jnp.float32, smallest / len(cuts), high / len(cuts)))
        loudness = loudness * jnp.repeat(draws, shape[dim] // blocks).reshape([-1 if axis == dim else 1 for axis in range(len(shape))])
    return loudness


def assign_block(own_key, own, number, rows, count, top, most, slope):
    order = jax.random.permutation(own_key, count)
    heavy_load, common = load_shares(count, rows * top, most, slope, True), load_shares(count, rows * top, most, slope, False)
    places = jnp.arange(count)

    def named(tallies, offset_by):
        used = int((tallies > 0).sum())
        fixed = max(1, used // 4)
        shifted = fixed + (places - fixed + offset_by * (used - fixed)) % max(1, count - fixed)
        return jnp.zeros((count,), jnp.int32).at[order[jnp.where(places < fixed, places, shifted)]].set(jnp.asarray(tallies, jnp.int32))

    tallies = jnp.where(number % 4 == 0, named(heavy_load, number // 4), named(common, number - number // 4 - 1))
    mixed = jax.random.permutation(jax.random.fold_in(own, 3), count)
    giver, receiver = mixed[0:count // 2 * 2:2], mixed[1:count // 2 * 2:2]
    room = jnp.minimum(tallies[giver] - 1, most - tallies[receiver]) // 2
    room = jnp.where((giver == order[0]) | (receiver == order[0]) | (tallies[receiver] == 0), 0, jnp.maximum(room, 0))
    shifted = jax.random.randint(jax.random.fold_in(own, 4), (count // 2,), 0, 1 << 20) % (room + 1)
    tallies = tallies.at[giver].add(-shifted).at[receiver].add(shifted)
    labels = jnp.searchsorted(jnp.cumsum(tallies), jnp.arange(rows * top), side="right").astype(jnp.int32)
    table = labels.reshape(top, rows).T
    table = table[jax.random.permutation(jax.random.fold_in(own, 1), rows)]
    offset_by = jax.random.randint(jax.random.fold_in(own, 2), (rows, 1), 0, top)
    return jnp.take_along_axis(table, (jnp.arange(top)[None, :] + offset_by) % top, axis=1)


def load_shares(amount, total, bound, skew, full):
    portions = [(1 << 20) // math.isqrt(rank ** skew) + 1 for rank in range(1, amount + 1)]
    largest = bound if full else min(bound, max(-(-total // amount), total * portions[0] // sum(portions)))
    least = 1 if total - largest >= amount - 1 else 0
    holding, rest = [largest] + [least] * (amount - 1), total - largest - least * (amount - 1)
    while rest > 0:
        movable = [i for i in range(1, amount) if holding[i] < largest] or [i for i in range(1, amount) if holding[i] < bound]
        mass, budget = sum([portions[i] for i in movable]), rest
        for i in movable:
            addition = min(bound - holding[i], max(1, budget * portions[i] // mass), rest)
            holding[i] = holding[i] + addition
            rest = rest - addition
    return np.array(holding)


def gaussian(own_key, dims, deviation, most, pieces=(), kind=jnp.bfloat16):
    drawn = jax.random.normal(own_key, dims, jnp.float32) * deviation
    if len(pieces) > 0:
        drawn = shard_levels(own_key, dims, pieces, -0.22, 0.18) * drawn
    return jnp.clip(drawn, min=-most, max=most).astype(kind)


def setup_inputs(seed: int = 0) -> dict:
    splits = jax.random.split(jax.random.key(seed), 9)
    elem_x = gaussian(splits[0], (N_KRING, N_KBLK, TILE, NG), 1.0, 6.0, ((0, 32), (1, 16)))
    elem_d = gaussian(splits[1], (N_KRING, N_KBLK, TILE, NGW), 1.0, 6.0, ((0, 32), (1, 16)))
    rows_x = gaussian(splits[2], (N_KRING, N_KBLK, TILE, NG), NG ** -0.5, 0.1875, ((0, 32), (1, 16)))
    rows_d = gaussian(splits[3], (N_KRING, N_KBLK, TILE, NGW), NGW ** -0.5, 0.25, ((0, 32), (1, 16)))
    coulomb = jnp.clip(jnp.exp(jax.random.uniform(splits[4], (NG,), jnp.float32, math.log(0.2), math.log(2.0))), 0.2, 2.0)
    screened = jnp.clip(jnp.exp(jax.random.uniform(splits[5], (NGW,), jnp.float32, math.log(0.1), math.log(1.0))), 0.1, 1.0)
    cutoff = plant(jax.random.randint(splits[6], (N_KRING, N_KBLK, N_KRING), NG // 4, NG + 1), jax.random.fold_in(splits[6], 1), NG // 4, NG).astype(jnp.int32)
    owners_keys = jax.random.split(jax.random.fold_in(splits[7], 1), N_KRING * N_KBLK * N_KRING // N_KRING)
    owners_turns = jax.random.permutation(jax.random.fold_in(splits[7], 3), N_KRING * N_KBLK * N_KRING // N_KRING)
    owners = jax.vmap(lambda own, number: assign_block(jax.random.fold_in(splits[7], 2), own, number, N_KRING, N_KBLK, 1, CAP, 2))(owners_keys, owners_turns).reshape((N_KRING, N_KBLK, N_KRING, 1))
    return dict(elem_x=elem_x, elem_d=elem_d, rows_x=rows_x, rows_d=rows_d, coulomb=coulomb, screened=screened, cutoff=cutoff, owners=owners)


def block_tiles(elem_one, elem_dir, column_x, column_d, coulomb, screened, cut_row):
    scaled_x = (elem_one.astype(jnp.float32) * coulomb).astype(jnp.bfloat16)
    scaled_d = (elem_dir.astype(jnp.float32) * screened).astype(jnp.bfloat16)
    g_index = jnp.arange(NG, dtype=jnp.int32)
    keep = g_index[None, None, :] < cut_row[:, None, None]
    masked = jnp.where(keep, column_x, jnp.zeros_like(column_x))
    exch_part = jnp.einsum('ng,bmg->bnm', scaled_x.astype(jnp.float32), masked.astype(jnp.float32))
    dir_part = jnp.einsum('ng,bmg->bnm', scaled_d.astype(jnp.float32), column_d.astype(jnp.float32))
    return (2.0 * exch_part - dir_part).astype(jnp.bfloat16)


def reference(elem_x, elem_d, rows_x, rows_d, coulomb, screened, cutoff, owners):
    def one_block(index):
        cycle_pos = index // N_KBLK
        blk_pos = index % N_KBLK
        return block_tiles(elem_x[cycle_pos, blk_pos], elem_d[cycle_pos, blk_pos], rows_x[:, blk_pos], rows_d[:, blk_pos], coulomb, screened, cutoff[cycle_pos, blk_pos])

    tile_set = lax.map(one_block, jnp.arange(N_KRING * N_KBLK, dtype=jnp.int32))
    tile_set = tile_set.reshape(N_KRING, N_KBLK, N_KRING, TILE, TILE)
    dest = owners[..., 0]
    onehot = (dest[..., None] == jnp.arange(N_KBLK, dtype=jnp.int32)).astype(jnp.int32)
    before = jnp.cumsum(onehot, axis=2) - onehot
    slot_of = jnp.sum(before * onehot, axis=-1).astype(jnp.int32)
    cycle_idx = jnp.broadcast_to(jnp.arange(N_KRING, dtype=jnp.int32)[:, None, None], dest.shape)
    blk_idx = jnp.broadcast_to(jnp.arange(N_KBLK, dtype=jnp.int32)[None, :, None], dest.shape)
    assembled = jnp.zeros((N_KRING, N_KBLK, N_KBLK, CAP, TILE, TILE), jnp.bfloat16)
    return assembled.at[cycle_idx, dest, blk_idx, slot_of].set(tile_set)
```

```python
import jax
import jax.numpy as jnp
from jax import lax
from jax.experimental import pallas as pl
from jax.experimental.pallas import tpu as pltpu
from jax.sharding import PartitionSpec as P

CAP = 4
RING = 8
PIECES = 2
LIST = 16


def place(i):
    return i // 4, (i // 2) % 2, i % 2


def index(y, z, c):
    return ((y % RING) * 2 + z) * 2 + c


def pairs(move):
    return [(i, index(*move(*place(i)))) for i in range(4 * RING)]


OTHER_CORE = pairs(lambda y, z, c: (y, z, 1 - c))
OTHER_HALF = pairs(lambda y, z, c: (y, 1 - z, c))
ONWARD = pairs(lambda y, z, c: (y + 1 - 2 * c, z, c))


def send(x, perm):
    return lax.ppermute(x, "kring", perm)


def tiles_kernel(cut_ref, elem_ref, *refs):
    *row_refs, out_ref, masked = refs
    g_count = 1024
    rows = out_ref.shape[1]
    lane = lax.broadcasted_iota(jnp.int32, (16, g_count), 1)
    at = 0
    for ref in row_refs:
        for k in range(ref.shape[0]):
            keep = (lane < cut_ref[at]).astype(jnp.float32).astype(jnp.bfloat16)
            part = ref[k, :, :g_count].reshape(rows // 16, 16, g_count) * keep[None]
            span = pl.ds(at * rows, rows)
            masked[span, :g_count] = part.reshape(rows, g_count)
            masked[span, g_count:] = ref[k, :, g_count:]
            at += 1
    total = jnp.dot(masked[...], elem_ref[...], preferred_element_type=jnp.float32)
    out_ref[...] = total.astype(jnp.bfloat16).reshape(out_ref.shape)


def make_tiles(cut, elem_t, blocks):
    rows, depth = blocks[0].shape[1:]
    width = elem_t.shape[1]
    vmem = pl.BlockSpec(memory_space=pltpu.VMEM)
    return pl.pallas_call(
        tiles_kernel,
        out_shape=jax.ShapeDtypeStruct((LIST, rows, width), jnp.bfloat16),
        in_specs=[pl.BlockSpec(memory_space=pltpu.SMEM)] + [vmem] * (1 + len(blocks)),
        out_specs=vmem,
        scratch_shapes=[pltpu.VMEM((LIST * rows, depth), jnp.bfloat16)],
        compiler_params=pltpu.CompilerParams(vmem_limit_bytes=40 << 20),
        cost_estimate=pl.CostEstimate(
            flops=2 * LIST * rows * depth * width, bytes_accessed=2 * LIST * rows * depth, transcendentals=0
        ),
    )(cut, elem_t, *blocks)


def outbox_kernel(pos_ref, mine_ref, other_ref, out_ref, held):
    held[:LIST] = mine_ref[...]
    held[LIST : 2 * LIST] = other_ref[...]
    held[2 * LIST] = jnp.zeros(held.shape[1:], held.dtype)
    for s in range(out_ref.shape[0]):
        out_ref[s] = held[pos_ref[s]]


def make_outbox(pos, mine, other):
    rows, width = mine.shape[1:]
    slots = pos.shape[0]
    vmem = pl.BlockSpec(memory_space=pltpu.VMEM)
    return pl.pallas_call(
        outbox_kernel,
        out_shape=jax.ShapeDtypeStruct((slots, rows, width), jnp.bfloat16),
        in_specs=[pl.BlockSpec(memory_space=pltpu.SMEM), vmem, vmem],
        out_specs=vmem,
        scratch_shapes=[pltpu.VMEM((2 * LIST + 1, rows, width), jnp.bfloat16)],
        compiler_params=pltpu.CompilerParams(vmem_limit_bytes=16 << 20),
    )(pos, mine, other)


def turn_kernel(*refs):
    *in_refs, out_ref = refs
    for s in range(out_ref.shape[0]):
        whole = jnp.concatenate([ref[s] for ref in in_refs], axis=0)
        out_ref[s] = whole.T


def turn(parts):
    slots, _, width = parts[0].shape
    rows = sum(p.shape[1] for p in parts)
    at_once = 8
    return pl.pallas_call(
        turn_kernel,
        grid=(slots // at_once,),
        out_shape=jax.ShapeDtypeStruct((slots, width, rows), jnp.bfloat16),
        in_specs=[pl.BlockSpec((at_once,) + p.shape[1:], lambda s: (s, 0, 0)) for p in parts],
        out_specs=pl.BlockSpec((at_once, width, rows), lambda s: (s, 0, 0)),
    )(*parts)


def body(elem_x, elem_d, rows_x, rows_d, coulomb, screened, cutoff, owners):
    blk_len = lax.axis_size("kblk")
    me = lax.axis_index("kring")
    my_y, my_z, my_c = place(me)
    rows = jnp.concatenate([rows_x[0, 0], rows_d[0, 0]], axis=1)
    tile_rows = rows.shape[0]
    step = tile_rows // PIECES

    near = send(rows, OTHER_CORE)
    far = [send(rows[k * step : (k + 1) * step], OTHER_HALF) for k in range(PIECES)]

    scaled_x = (elem_x[0, 0].astype(jnp.float32) * coulomb).astype(jnp.bfloat16)
    scaled_d = (elem_d[0, 0].astype(jnp.float32) * screened).astype(jnp.bfloat16)
    elem_t = jnp.concatenate([2 * scaled_x, -scaled_d], axis=1).T
    cut_row = cutoff[0, 0]
    elem_near = send(elem_t, OTHER_CORE)
    cut_near = send(cut_row, OTHER_CORE)

    partner = jnp.arange(4 * RING, dtype=jnp.int32)
    p_y, p_z, p_c = place(partner)

    def in_list(core):
        ahead = jnp.where(core == 0, my_y - p_y, p_y - my_y) % RING
        off = jnp.abs(p_c - core)
        has = jnp.where((ahead == 0) | (ahead == 4), off == 0, ahead < 4)
        spot = jnp.where(ahead == 0, 0, 2 * ahead - 1 + off) + 8 * jnp.abs(p_z - my_z)
        return has, spot

    has_mine, spot_mine = in_list(my_c)
    _, spot_other = in_list(1 - my_c)
    spot = jnp.where(has_mine, spot_mine, LIST + spot_other)
    fits = has_mine[None, :] & (spot_mine[None, :] == jnp.arange(LIST, dtype=jnp.int32)[:, None])
    cut_mine = jnp.sum(jnp.where(fits, cut_row[None, :], 0), axis=1)
    cut_other = jnp.sum(jnp.where(fits, cut_near[None, :], 0), axis=1)

    dest = owners[0, 0, :, 0]
    same = (dest[:, None] == dest[None, :]) & (partner[None, :] < partner[:, None])
    slot_of = jnp.sum(same.astype(jnp.int32), axis=1)
    slots = jnp.arange(blk_len * CAP, dtype=jnp.int32)
    hit = slots[:, None] == (dest * CAP + slot_of)[None, :]
    pos = 2 * LIST + jnp.sum(jnp.where(hit, (spot - 2 * LIST)[None, :], 0), axis=1)

    received = []
    for k in range(PIECES):
        span = slice(k * step, (k + 1) * step)
        blocks = []
        for first, second in ((rows[span], near[span]), (far[k], send(far[k], OTHER_CORE))):
            held = jnp.stack([first, second])
            blocks.append(held[:1])
            for _ in range(3):
                held = send(held, ONWARD)
                blocks.append(held)
            blocks.append(send(held[:1], ONWARD))
        other = send(make_tiles(cut_other, elem_near, blocks), OTHER_CORE)
        mine = make_tiles(cut_mine, elem_t, blocks)
        outbox = make_outbox(pos, mine, other).reshape(blk_len, CAP, step, tile_rows)
        got = lax.all_to_all(outbox, "kblk", split_axis=0, concat_axis=0, tiled=True)
        received.append(got.reshape(blk_len * CAP, step, tile_rows))
    return turn(received).reshape(1, 1, blk_len, CAP, tile_rows, tile_rows)


def solution(mesh):
    in_specs = (
        P("kring", "kblk", None, None),
        P("kring", "kblk", None, None),
        P("kring", "kblk", None, None),
        P("kring", "kblk", None, None),
        P(),
        P(),
        P("kring", "kblk", None),
        P("kring", "kblk", None, None),
    )
    out_specs = P("kring", "kblk", None, None, None, None)
    return jax.shard_map(body, mesh=mesh, in_specs=in_specs, out_specs=out_specs, check_vma=False)
```

```python
import functools

import jax
import jax.numpy as jnp
from jax import lax
from jax.experimental import pallas as pl
from jax.experimental.pallas import tpu as pltpu
from jax.sharding import PartitionSpec as P

CAP = 4
RING = 8
TILE = 128
G_COUNT = 1024
OWN_CHAINS = 2
FAR_CHAINS = 2


def place(i):
    return i // 4, (i // 2) % 2, i % 2


def index(y, z, c):
    return ((y % RING) * 2 + z) * 2 + c


def pairs(move):
    return [(i, index(*move(*place(i)))) for i in range(4 * RING)]


OTHER_CORE = pairs(lambda y, z, c: (y, z, 1 - c))
OTHER_HALF = pairs(lambda y, z, c: (y, 1 - z, c))
ONWARD = pairs(lambda y, z, c: (y + 1 - 2 * c, z, c))


def send(x, perm):
    return lax.ppermute(x, "kring", perm)


def tiles_kernel(count, cut_ref, elem_ref, *refs):
    *block_refs, out_ref, masked, total = refs
    depth = masked.shape[1]
    lane = lax.broadcasted_iota(jnp.int32, (16, G_COUNT), 1)
    half = len(block_refs) // count
    for first in range(count):
        refs_here = block_refs[first::count]
        rows = refs_here[0].shape[1]
        at = 0
        for j, ref in enumerate(refs_here):
            for k in range(1 if j in (0, half - 1) else 2):
                keep = (lane < cut_ref[at]).astype(jnp.float32).astype(jnp.bfloat16)
                part = ref[k, :, :G_COUNT].reshape(rows // 16, 16, G_COUNT) * keep[None]
                span = pl.ds(at * TILE + first * rows, rows)
                masked[span, :G_COUNT] = part.reshape(rows, G_COUNT)
                masked[span, G_COUNT:] = ref[k, :, G_COUNT:]
                at += 1
    total[...] = jnp.dot(masked[...], elem_ref[:depth, :], preferred_element_type=jnp.float32)
    for k in range(RING):
        out_ref[k] = total[pl.ds(k * TILE, TILE), :].T.astype(jnp.bfloat16)


def make_tiles(cuts, elem, blocks, after=()):
    depth = blocks[0][0].shape[2]
    flat = [b for step in zip(*blocks) for b in step]
    vmem = pl.BlockSpec(memory_space=pltpu.VMEM)
    free = pl.BlockSpec(memory_space=pl.ANY)

    def kernel(*refs):
        tiles_kernel(len(blocks), *refs[: 2 + len(flat)], *refs[2 + len(flat) + len(after) :])

    return pl.pallas_call(
        kernel,
        out_shape=jax.ShapeDtypeStruct((RING, TILE, TILE), jnp.bfloat16),
        in_specs=[pl.BlockSpec(memory_space=pltpu.SMEM)] + [vmem] * (1 + len(flat)) + [free] * len(after),
        out_specs=vmem,
        scratch_shapes=[
            pltpu.VMEM((RING * TILE, depth), jnp.bfloat16),
            pltpu.VMEM((RING * TILE, TILE), jnp.float32),
        ],
        compiler_params=pltpu.CompilerParams(vmem_limit_bytes=24 << 20),
        cost_estimate=pl.CostEstimate(
            flops=2 * RING * TILE * depth * TILE, bytes_accessed=2 * RING * TILE * depth, transcendentals=0
        ),
    )(cuts, elem, *flat, *after)


def pair_kernel(pieces, a_ref, b_ref, *refs):
    out_refs = refs[-pieces:]
    rows = out_refs[0].shape[1]
    for k, ref in enumerate(out_refs):
        ref[0] = a_ref[pl.ds(k * rows, rows), :]
        ref[1] = b_ref[pl.ds(k * rows, rows), :]


def pair(a, b, pieces, after=()):
    vmem = pl.BlockSpec(memory_space=pltpu.VMEM)
    free = pl.BlockSpec(memory_space=pl.ANY)
    shape = jax.ShapeDtypeStruct((2, a.shape[0] // pieces, a.shape[1]), a.dtype)
    return pl.pallas_call(
        functools.partial(pair_kernel, pieces),
        out_shape=(shape,) * pieces,
        in_specs=[vmem, vmem] + [free] * len(after),
        out_specs=(vmem,) * pieces,
        compiler_params=pltpu.CompilerParams(vmem_limit_bytes=8 << 20),
    )(a, b, *after)


def outbox_kernel(pos_ref, *refs):
    in_refs, (out_ref, held) = refs[:4], refs[-2:]
    for k, ref in enumerate(in_refs):
        held[k * RING : (k + 1) * RING] = ref[...]
    held[4 * RING] = jnp.zeros(held.shape[1:], held.dtype)
    for s in range(out_ref.shape[0]):
        out_ref[s] = held[pos_ref[s]]


def make_outbox(pos, parts, after=()):
    rows, width = parts[0].shape[1:]
    slots = pos.shape[0]
    free = pl.BlockSpec(memory_space=pl.ANY)
    vmem = pl.BlockSpec(memory_space=pltpu.VMEM)
    return pl.pallas_call(
        outbox_kernel,
        out_shape=jax.ShapeDtypeStruct((slots, rows, width), jnp.bfloat16),
        in_specs=[pl.BlockSpec(memory_space=pltpu.SMEM)] + [vmem] * 4 + [free] * len(after),
        out_specs=vmem,
        scratch_shapes=[pltpu.VMEM((4 * RING + 1, rows, width), jnp.bfloat16)],
        compiler_params=pltpu.CompilerParams(vmem_limit_bytes=16 << 20),
    )(pos, *parts, *after)


def copy_kernel(x_ref, *refs):
    refs[-1][...] = x_ref[...]


def copy_after(x, after):
    vmem = pl.BlockSpec(memory_space=pltpu.VMEM)
    free = pl.BlockSpec(memory_space=pl.ANY)
    return pl.pallas_call(
        copy_kernel,
        out_shape=jax.ShapeDtypeStruct(x.shape, x.dtype),
        in_specs=[vmem] + [free] * len(after),
        out_specs=vmem,
        compiler_params=pltpu.CompilerParams(vmem_limit_bytes=8 << 20),
    )(x, *after)


def ring(held):
    blocks = [held]
    for _ in range(RING // 2 - 1):
        held = send(held, ONWARD)
        blocks.append(held)
    return blocks + [send(held[:1], ONWARD)]


def body(elem_x, elem_d, rows_x, rows_d, coulomb, screened, cutoff, owners):
    blk_len = lax.axis_size("kblk")
    me = lax.axis_index("kring")
    my_y, my_z, my_c = place(me)
    rows = jnp.concatenate([rows_x[0, 0], rows_d[0, 0]], axis=1)
    tile_rows, depth = rows.shape

    scaled_x = (elem_x[0, 0].astype(jnp.float32) * coulomb).astype(jnp.bfloat16)
    scaled_d = (elem_d[0, 0].astype(jnp.float32) * screened).astype(jnp.bfloat16)
    cut = cutoff[0, 0]
    cut_parts = jnp.stack([cut // 32, cut % 32]).astype(jnp.bfloat16)
    cut_parts = jnp.pad(cut_parts, ((0, 14), (0, tile_rows - cut.shape[0])))
    elem_t = jnp.concatenate([2 * scaled_x, -scaled_d], axis=1).T
    elem_t = jnp.concatenate([elem_t, cut_parts])
    near = send(elem_t, OTHER_CORE)

    far = send(rows, OTHER_HALF)
    near_rows = send(copy_after(rows, (elem_t,)), OTHER_CORE)
    own = [ring(held) for held in pair(rows, near_rows, OWN_CHAINS)]
    early = [chain[1] for chain in own]
    far = copy_after(far, early)
    far = [ring(held) for held in pair(far, send(far, OTHER_CORE), FAR_CHAINS)]


    partner = jnp.arange(4 * RING, dtype=jnp.int32)
    p_y, p_z, p_c = place(partner)

    def in_list(core):
        ahead = jnp.where(core == 0, my_y - p_y, p_y - my_y) % RING
        off = jnp.abs(p_c - core)
        has = jnp.where((ahead == 0) | (ahead == 4), off == 0, ahead < 4)
        return has, jnp.where(ahead == 0, 0, 2 * ahead - 1 + off)

    has_mine, spot_mine = in_list(my_c)
    _, spot_other = in_list(1 - my_c)
    listed = has_mine & (spot_mine == jnp.arange(RING, dtype=jnp.int32)[:, None])

    def cuts_of(elem, z):
        parts = elem[depth : depth + 2, : 4 * RING].astype(jnp.int32)
        row = parts[0] * 32 + parts[1]
        return jnp.sum(jnp.where(listed & (p_z == z), row[None, :], 0), axis=1)


    spot = jnp.where(has_mine, spot_mine, RING + spot_other) + 2 * RING * jnp.abs(p_z - my_z)
    dest = owners[0, 0, :, 0]
    same = (dest[:, None] == dest[None, :]) & (partner[None, :] < partner[:, None])
    slot_of = jnp.sum(same.astype(jnp.int32), axis=1)
    slots = jnp.arange(blk_len * CAP, dtype=jnp.int32)
    hit = slots[:, None] == (dest * CAP + slot_of)[None, :]
    pos = 4 * RING + jnp.sum(jnp.where(hit, (spot - 4 * RING)[None, :], 0), axis=1)

    parts = []
    for blocks, z in ((own, my_z), (far, 1 - my_z)):
        to_near = make_tiles(cuts_of(near, z), near, blocks)
        parts.append(make_tiles(cuts_of(elem_t, z), elem_t, blocks))
        parts.append(send(to_near, OTHER_CORE))
    outbox = make_outbox(pos, parts).reshape(blk_len, CAP, tile_rows, tile_rows)
    received = lax.all_to_all(outbox, "kblk", split_axis=0, concat_axis=0, tiled=True)
    return received[None, None]


def solution(mesh):
    in_specs = (
        P("kring", "kblk", None, None),
        P("kring", "kblk", None, None),
        P("kring", "kblk", None, None),
        P("kring", "kblk", None, None),
        P(),
        P(),
        P("kring", "kblk", None),
        P("kring", "kblk", None, None),
    )
    out_specs = P("kring", "kblk", None, None, None, None)
    return jax.shard_map(body, mesh=mesh, in_specs=in_specs, out_specs=out_specs, check_vma=False)
```

```python
import functools

import jax
import jax.numpy as jnp
from jax import lax
from jax.experimental import pallas as pl
from jax.experimental.pallas import tpu as pltpu
from jax.sharding import PartitionSpec as P

CAP = 4
RING = 8
TILE = 128
G_COUNT = 1024
CHAINS = 2
STEPS = ((0, 1, 2, 3, 4),)


def place(i):
    return i // 4, (i // 2) % 2, i % 2


def index(y, z, c):
    return ((y % RING) * 2 + z) * 2 + c


def pairs(move):
    return [(i, index(*move(*place(i)))) for i in range(4 * RING)]


OTHER_CORE = pairs(lambda y, z, c: (y, z, 1 - c))
OTHER_HALF = pairs(lambda y, z, c: (y, 1 - z, c))
OTHER_BOTH = pairs(lambda y, z, c: (y, 1 - z, 1 - c))
ONWARD = pairs(lambda y, z, c: (y + 1 - 2 * c, z, c))


def send(x, perm):
    return lax.ppermute(x, "kring", perm)


def tiles_kernel(parts, cut_ref, elem_a, elem_b, *refs):
    *block_refs, out_a, out_b, masked, total = refs
    depth = masked.shape[2]
    lane = lax.broadcasted_iota(jnp.int32, (16, G_COUNT), 1)
    for e, (elem_ref, out_ref) in enumerate(((elem_a, out_a), (elem_b, out_b))):
        for at, (spot, sources, k) in enumerate(parts):
            keep = (lane < cut_ref[e, spot]).astype(jnp.float32).astype(jnp.bfloat16)
            for n, source in enumerate(sources):
                ref = block_refs[source]
                rows = ref.shape[1]
                part = ref[k, :, :G_COUNT].reshape(rows // 16, 16, G_COUNT) * keep[None]
                span = pl.ds(at * TILE + n * rows, rows)
                masked[e, span, :G_COUNT] = part.reshape(rows, G_COUNT)
                masked[e, span, G_COUNT:] = ref[k, :, G_COUNT:]
        total[e] = jnp.dot(masked[e], elem_ref[:depth, :], preferred_element_type=jnp.float32)
        for at in range(len(parts)):
            out_ref[at] = total[e, pl.ds(at * TILE, TILE), :].T.astype(jnp.bfloat16)


def make_tiles(cuts, elem_a, elem_b, chains, steps, after=()):
    depth = chains[0][0].shape[2]
    flat, parts = [], []
    for step in steps:
        sources = list(range(len(flat), len(flat) + len(chains)))
        flat += [chain[step] for chain in chains]
        for k in range(1 if step in (0, RING // 2) else 2):
            parts.append((max(0, 2 * step - 1) + k, sources, k))
    vmem = pl.BlockSpec(memory_space=pltpu.VMEM)
    free = pl.BlockSpec(memory_space=pl.ANY)
    count = len(parts)
    shape = jax.ShapeDtypeStruct((count, TILE, TILE), jnp.bfloat16)

    def kernel(*refs):
        tiles_kernel(parts, *refs[: 3 + len(flat)], *refs[3 + len(flat) + len(after) :])

    return pl.pallas_call(
        kernel,
        out_shape=(shape, shape),
        in_specs=[pl.BlockSpec(memory_space=pltpu.SMEM)] + [vmem] * (2 + len(flat)) + [free] * len(after),
        out_specs=(vmem, vmem),
        scratch_shapes=[
            pltpu.VMEM((2, count * TILE, depth), jnp.bfloat16),
            pltpu.VMEM((2, count * TILE, TILE), jnp.float32),
        ],
        compiler_params=pltpu.CompilerParams(vmem_limit_bytes=24 << 20),
        cost_estimate=pl.CostEstimate(
            flops=4 * count * TILE * depth * TILE, bytes_accessed=2 * count * TILE * depth, transcendentals=0
        ),
    )(cuts, elem_a, elem_b, *flat, *after)


def pair_kernel(pieces, a_ref, b_ref, *refs):
    out_refs = refs[-pieces:]
    rows = out_refs[0].shape[1]
    for k, ref in enumerate(out_refs):
        ref[0] = a_ref[pl.ds(k * rows, rows), :]
        ref[1] = b_ref[pl.ds(k * rows, rows), :]


def pair(a, b, pieces, after=()):
    vmem = pl.BlockSpec(memory_space=pltpu.VMEM)
    free = pl.BlockSpec(memory_space=pl.ANY)
    shape = jax.ShapeDtypeStruct((2, a.shape[0] // pieces, a.shape[1]), a.dtype)
    return pl.pallas_call(
        functools.partial(pair_kernel, pieces),
        out_shape=(shape,) * pieces,
        in_specs=[vmem, vmem] + [free] * len(after),
        out_specs=(vmem,) * pieces,
        compiler_params=pltpu.CompilerParams(vmem_limit_bytes=8 << 20),
    )(a, b, *after)


def outbox_kernel(pos_ref, *refs):
    *in_refs, out_ref, held = refs
    at = 0
    for ref in in_refs:
        held[at : at + ref.shape[0]] = ref[...]
        at += ref.shape[0]
    held[at] = jnp.zeros(held.shape[1:], held.dtype)
    for s in range(out_ref.shape[0]):
        out_ref[s] = held[pos_ref[s]]


def make_outbox(pos, parts):
    rows, width = parts[0].shape[1:]
    slots = pos.shape[0]
    vmem = pl.BlockSpec(memory_space=pltpu.VMEM)
    return pl.pallas_call(
        outbox_kernel,
        out_shape=jax.ShapeDtypeStruct((slots, rows, width), jnp.bfloat16),
        in_specs=[pl.BlockSpec(memory_space=pltpu.SMEM)] + [vmem] * len(parts),
        out_specs=vmem,
        scratch_shapes=[pltpu.VMEM((4 * RING + 1, rows, width), jnp.bfloat16)],
        compiler_params=pltpu.CompilerParams(vmem_limit_bytes=16 << 20),
    )(pos, *parts)


def copy_kernel(x_ref, *refs):
    refs[-1][...] = x_ref[...]


def copy_after(x, after):
    vmem = pl.BlockSpec(memory_space=pltpu.VMEM)
    free = pl.BlockSpec(memory_space=pl.ANY)
    return pl.pallas_call(
        copy_kernel,
        out_shape=jax.ShapeDtypeStruct(x.shape, x.dtype),
        in_specs=[vmem] + [free] * len(after),
        out_specs=vmem,
        compiler_params=pltpu.CompilerParams(vmem_limit_bytes=8 << 20),
    )(x, *after)


def ring(held):
    blocks = [held]
    for _ in range(RING // 2 - 1):
        held = send(held, ONWARD)
        blocks.append(held)
    return blocks + [send(held[:1], ONWARD)]


def body(elem_x, elem_d, rows_x, rows_d, coulomb, screened, cutoff, owners):
    blk_len = lax.axis_size("kblk")
    me = lax.axis_index("kring")
    my_y, my_z, my_c = place(me)
    rows = jnp.concatenate([rows_x[0, 0], rows_d[0, 0]], axis=1)
    tile_rows, depth = rows.shape

    chains = [ring(held) for held in pair(rows, send(rows, OTHER_CORE), CHAINS)]

    scaled_x = (elem_x[0, 0].astype(jnp.float32) * coulomb).astype(jnp.bfloat16)
    scaled_d = (elem_d[0, 0].astype(jnp.float32) * screened).astype(jnp.bfloat16)
    cut = cutoff[0, 0]
    cut_parts = jnp.stack([cut // 32, cut % 32]).astype(jnp.bfloat16)
    cut_parts = jnp.pad(cut_parts, ((0, 14), (0, tile_rows - cut.shape[0])))
    elem_t = jnp.concatenate([2 * scaled_x, -scaled_d], axis=1).T
    elem_t = jnp.concatenate([elem_t, cut_parts])
    far = send(elem_t, OTHER_HALF)
    far = copy_after(far, (chains[0][3],))
    far_near = send(far, OTHER_CORE)
    near = send(elem_t, OTHER_CORE)

    partner = jnp.arange(4 * RING, dtype=jnp.int32)
    p_y, p_z, p_c = place(partner)

    def in_list(core):
        ahead = jnp.where(core == 0, my_y - p_y, p_y - my_y) % RING
        off = jnp.abs(p_c - core)
        has = jnp.where((ahead == 0) | (ahead == 4), off == 0, ahead < 4)
        return has, jnp.where(ahead == 0, 0, 2 * ahead - 1 + off)

    has_mine, spot_mine = in_list(my_c)
    _, spot_other = in_list(1 - my_c)
    listed = has_mine & (p_z == my_z) & (spot_mine == jnp.arange(RING, dtype=jnp.int32)[:, None])

    def cuts_of(*elems):
        parts = jnp.stack([e[depth : depth + 2, : 4 * RING] for e in elems]).astype(jnp.int32)
        row = parts[:, 0] * 32 + parts[:, 1]
        return jnp.sum(jnp.where(listed[None], row[:, None, :], 0), axis=2)

    cuts_far, cuts_near = cuts_of(far, far_near), cuts_of(elem_t, near)

    spot = jnp.where(has_mine, spot_mine, RING + spot_other) + 2 * RING * jnp.abs(p_z - my_z)
    dest = owners[0, 0, :, 0]
    same = (dest[:, None] == dest[None, :]) & (partner[None, :] < partner[:, None])
    slot_of = jnp.sum(same.astype(jnp.int32), axis=1)
    slots = jnp.arange(blk_len * CAP, dtype=jnp.int32)
    hit = slots[:, None] == (dest * CAP + slot_of)[None, :]
    pos = 4 * RING + jnp.sum(jnp.where(hit, (spot - 4 * RING)[None, :], 0), axis=1)

    from_far, from_far_near, after = [], [], ()
    for steps in STEPS:
        to_far, to_far_near = make_tiles(cuts_far, far, far_near, chains, steps, after)
        from_far.append(send(to_far, OTHER_HALF))
        from_far_near.append(send(to_far_near, OTHER_BOTH))
        after = from_far[-1:]
    mine, to_near = make_tiles(cuts_near, elem_t, near, chains, range(RING // 2 + 1), (to_far,))
    parts = [mine, send(to_near, OTHER_CORE)] + from_far + from_far_near
    outbox = make_outbox(pos, parts).reshape(blk_len, CAP, tile_rows, tile_rows)
    received = lax.all_to_all(outbox, "kblk", split_axis=0, concat_axis=0, tiled=True)
    return received[None, None]


def solution(mesh):
    in_specs = (
        P("kring", "kblk", None, None),
        P("kring", "kblk", None, None),
        P("kring", "kblk", None, None),
        P("kring", "kblk", None, None),
        P(),
        P(),
        P("kring", "kblk", None),
        P("kring", "kblk", None, None),
    )
    out_specs = P("kring", "kblk", None, None, None, None)
    return jax.shard_map(body, mesh=mesh, in_specs=in_specs, out_specs=out_specs, check_vma=False)
```

```python
import functools

import jax
import jax.numpy as jnp
from jax import lax
from jax.experimental import pallas as pl
from jax.experimental.pallas import tpu as pltpu
from jax.sharding import PartitionSpec as P

CAP = 4
RING = 8
TILE = 128
G_COUNT = 1024
CHAINS = 2


def place(i):
    return i // 4, (i // 2) % 2, i % 2


def index(y, z, c):
    return ((y % RING) * 2 + z) * 2 + c


def pairs(move):
    return [(i, index(*move(*place(i)))) for i in range(4 * RING)]


OTHER_CORE = pairs(lambda y, z, c: (y, z, 1 - c))
OTHER_HALF = pairs(lambda y, z, c: (y, 1 - z, c))
OTHER_BOTH = pairs(lambda y, z, c: (y, 1 - z, 1 - c))
ONWARD = pairs(lambda y, z, c: (y + 1 - 2 * c, z, c))


def send(x, perm):
    return lax.ppermute(x, "kring", perm)


def tiles_kernel(parts, count, cut_ref, *refs):
    elem_refs, block_refs, out_refs = refs[:count], refs[count : -count - 2], refs[-count - 2 : -2]
    masked, total = refs[-2:]
    depth = masked.shape[2]
    lane = lax.broadcasted_iota(jnp.int32, (16, G_COUNT), 1)
    for e, (elem_ref, out_ref) in enumerate(zip(elem_refs, out_refs)):
        for at, (spot, sources, k) in enumerate(parts):
            keep = (lane < cut_ref[e, spot]).astype(jnp.float32).astype(jnp.bfloat16)
            for n, source in enumerate(sources):
                ref = block_refs[source]
                rows = ref.shape[1]
                part = ref[k, :, :G_COUNT].reshape(rows // 16, 16, G_COUNT) * keep[None]
                span = pl.ds(at * TILE + n * rows, rows)
                masked[e, span, :G_COUNT] = part.reshape(rows, G_COUNT)
                masked[e, span, G_COUNT:] = ref[k, :, G_COUNT:]
        total[e] = jnp.dot(masked[e], elem_ref[:depth, :], preferred_element_type=jnp.float32)
        for at in range(len(parts)):
            out_ref[at] = total[e, pl.ds(at * TILE, TILE), :].T.astype(jnp.bfloat16)


def make_tiles(cuts, elems, chains, steps, after=()):
    depth = chains[0][0].shape[2]
    flat, parts = [], []
    for step in steps:
        sources = list(range(len(flat), len(flat) + len(chains)))
        flat += [chain[step] for chain in chains]
        for k in range(1 if step in (0, RING // 2) else 2):
            parts.append((max(0, 2 * step - 1) + k, sources, k))
    vmem = pl.BlockSpec(memory_space=pltpu.VMEM)
    free = pl.BlockSpec(memory_space=pl.ANY)
    count = len(parts)
    shape = jax.ShapeDtypeStruct((count, TILE, TILE), jnp.bfloat16)

    def kernel(*refs):
        read = 1 + len(elems) + len(flat)
        tiles_kernel(parts, len(elems), *refs[:read], *refs[read + len(after) :])

    return pl.pallas_call(
        kernel,
        out_shape=(shape,) * len(elems),
        in_specs=[pl.BlockSpec(memory_space=pltpu.SMEM)] + [vmem] * (len(elems) + len(flat)) + [free] * len(after),
        out_specs=(vmem,) * len(elems),
        scratch_shapes=[
            pltpu.VMEM((len(elems), count * TILE, depth), jnp.bfloat16),
            pltpu.VMEM((len(elems), count * TILE, TILE), jnp.float32),
        ],
        compiler_params=pltpu.CompilerParams(vmem_limit_bytes=24 << 20),
        cost_estimate=pl.CostEstimate(
            flops=2 * len(elems) * count * TILE * depth * TILE, bytes_accessed=2 * count * TILE * depth, transcendentals=0
        ),
    )(cuts, *elems, *flat, *after)


def pair_kernel(pieces, a_ref, b_ref, *refs):
    out_refs = refs[-pieces:]
    rows = out_refs[0].shape[1]
    for k, ref in enumerate(out_refs):
        ref[0] = a_ref[pl.ds(k * rows, rows), :]
        ref[1] = b_ref[pl.ds(k * rows, rows), :]


def pair(a, b, pieces, after=()):
    vmem = pl.BlockSpec(memory_space=pltpu.VMEM)
    free = pl.BlockSpec(memory_space=pl.ANY)
    shape = jax.ShapeDtypeStruct((2, a.shape[0] // pieces, a.shape[1]), a.dtype)
    return pl.pallas_call(
        functools.partial(pair_kernel, pieces),
        out_shape=(shape,) * pieces,
        in_specs=[vmem, vmem] + [free] * len(after),
        out_specs=(vmem,) * pieces,
        compiler_params=pltpu.CompilerParams(vmem_limit_bytes=8 << 20),
    )(a, b, *after)


def outbox_kernel(pos_ref, *refs):
    *in_refs, out_ref, held = refs
    at = 0
    for ref in in_refs:
        held[at : at + ref.shape[0]] = ref[...]
        at += ref.shape[0]
    held[at] = jnp.zeros(held.shape[1:], held.dtype)
    for s in range(out_ref.shape[0]):
        out_ref[s] = held[pos_ref[s]]


def make_outbox(pos, parts):
    rows, width = parts[0].shape[1:]
    slots = pos.shape[0]
    vmem = pl.BlockSpec(memory_space=pltpu.VMEM)
    return pl.pallas_call(
        outbox_kernel,
        out_shape=jax.ShapeDtypeStruct((slots, rows, width), jnp.bfloat16),
        in_specs=[pl.BlockSpec(memory_space=pltpu.SMEM)] + [vmem] * len(parts),
        out_specs=vmem,
        scratch_shapes=[pltpu.VMEM((4 * RING + 1, rows, width), jnp.bfloat16)],
        compiler_params=pltpu.CompilerParams(vmem_limit_bytes=16 << 20),
    )(pos, *parts)


def copy_kernel(x_ref, *refs):
    refs[-1][...] = x_ref[...]


def copy_after(x, after):
    vmem = pl.BlockSpec(memory_space=pltpu.VMEM)
    free = pl.BlockSpec(memory_space=pl.ANY)
    return pl.pallas_call(
        copy_kernel,
        out_shape=jax.ShapeDtypeStruct(x.shape, x.dtype),
        in_specs=[vmem] + [free] * len(after),
        out_specs=vmem,
        compiler_params=pltpu.CompilerParams(vmem_limit_bytes=8 << 20),
    )(x, *after)


def ring(held):
    blocks = [held]
    for _ in range(RING // 2 - 1):
        held = send(held, ONWARD)
        blocks.append(held)
    return blocks + [send(held[:1], ONWARD)]


def body(elem_x, elem_d, rows_x, rows_d, coulomb, screened, cutoff, owners):
    blk_len = lax.axis_size("kblk")
    me = lax.axis_index("kring")
    my_y, my_z, my_c = place(me)
    rows = jnp.concatenate([rows_x[0, 0], rows_d[0, 0]], axis=1)
    tile_rows, depth = rows.shape

    held = pair(rows, send(rows, OTHER_CORE), CHAINS)
    chains = [ring(h) for h in held]

    scaled_x = (elem_x[0, 0].astype(jnp.float32) * coulomb).astype(jnp.bfloat16)
    scaled_d = (elem_d[0, 0].astype(jnp.float32) * screened).astype(jnp.bfloat16)
    cut = cutoff[0, 0]
    cut_parts = jnp.stack([cut // 32, cut % 32]).astype(jnp.bfloat16)
    cut_parts = jnp.pad(cut_parts, ((0, 14), (0, tile_rows - cut.shape[0])))
    elem_t = jnp.concatenate([2 * scaled_x, -scaled_d], axis=1).T
    elem_t = jnp.concatenate([elem_t, cut_parts])
    far = send(elem_t, OTHER_HALF)
    far = copy_after(far, (chains[0][3],))
    far_near = send(far, OTHER_CORE)

    partner = jnp.arange(4 * RING, dtype=jnp.int32)
    p_y, p_z, p_c = place(partner)

    def in_list(core):
        ahead = jnp.where(core == 0, my_y - p_y, p_y - my_y) % RING
        off = jnp.abs(p_c - core)
        has = jnp.where((ahead == 0) | (ahead == 4), off == 0, ahead < 4)
        return has, jnp.where(ahead == 0, 0, 2 * ahead - 1 + off)

    has_mine, spot_mine = in_list(my_c)
    _, spot_other = in_list(1 - my_c)
    listed = has_mine & (p_z == my_z) & (spot_mine == jnp.arange(RING, dtype=jnp.int32)[:, None])

    def cuts_of(*elems):
        parts = jnp.stack([e[depth : depth + 2, : 4 * RING] for e in elems]).astype(jnp.int32)
        row = parts[:, 0] * 32 + parts[:, 1]
        return jnp.sum(jnp.where(listed[None], row[:, None, :], 0), axis=2)

    cuts_far, cuts_far_near = cuts_of(far), cuts_of(far_near)

    spot = jnp.where(has_mine, spot_mine, RING + spot_other) + 2 * RING * jnp.abs(p_z - my_z)
    dest = owners[0, 0, :, 0]
    same = (dest[:, None] == dest[None, :]) & (partner[None, :] < partner[:, None])
    slot_of = jnp.sum(same.astype(jnp.int32), axis=1)
    slots = jnp.arange(blk_len * CAP, dtype=jnp.int32)
    hit = slots[:, None] == (dest * CAP + slot_of)[None, :]
    pos = 4 * RING + jnp.sum(jnp.where(hit, (spot - 4 * RING)[None, :], 0), axis=1)

    steps = range(RING // 2 + 1)
    (to_far_near,) = make_tiles(cuts_far_near, (far_near,), chains, steps)
    from_far_near = send(to_far_near, OTHER_BOTH)
    (to_far,) = make_tiles(cuts_far, (far,), chains, steps, (to_far_near,))
    from_far = send(to_far, OTHER_HALF)
    near = send(copy_after(elem_t, (chains[1][3],)), OTHER_CORE)
    cuts_near = cuts_of(elem_t, near)
    mine, to_near = make_tiles(cuts_near, (elem_t, near), chains, steps, (to_far,))
    parts = [mine, send(to_near, OTHER_CORE), from_far, from_far_near]
    outbox = make_outbox(pos, parts).reshape(blk_len, CAP, tile_rows, tile_rows)
    received = lax.all_to_all(outbox, "kblk", split_axis=0, concat_axis=0, tiled=True)
    return received[None, None]


def solution(mesh):
    in_specs = (
        P("kring", "kblk", None, None),
        P("kring", "kblk", None, None),
        P("kring", "kblk", None, None),
        P("kring", "kblk", None, None),
        P(),
        P(),
        P("kring", "kblk", None),
        P("kring", "kblk", None, None),
    )
    out_specs = P("kring", "kblk", None, None, None, None)
    return jax.shard_map(body, mesh=mesh, in_specs=in_specs, out_specs=out_specs, check_vma=False)
```

```python
import functools

import jax
import jax.numpy as jnp
from jax import lax
from jax.experimental import pallas as pl
from jax.experimental.pallas import tpu as pltpu
from jax.sharding import PartitionSpec as P

CAP = 4
RING = 8
TILE = 128
G_COUNT = 1024
CHAINS = 2


def place(i):
    return i // 4, (i // 2) % 2, i % 2


def index(y, z, c):
    return ((y % RING) * 2 + z) * 2 + c


def pairs(move):
    return [(i, index(*move(*place(i)))) for i in range(4 * RING)]


OTHER_CORE = pairs(lambda y, z, c: (y, z, 1 - c))
OTHER_HALF = pairs(lambda y, z, c: (y, 1 - z, c))
OTHER_BOTH = pairs(lambda y, z, c: (y, 1 - z, 1 - c))
ONWARD = pairs(lambda y, z, c: (y + 1 - 2 * c, z, c))


def send(x, perm):
    return lax.ppermute(x, "kring", perm)


def tiles_kernel(parts, count, cut_ref, *refs):
    elem_refs, block_refs, out_refs = refs[:count], refs[count : -count - 2], refs[-count - 2 : -2]
    masked, total = refs[-2:]
    depth = masked.shape[2]
    lane = lax.broadcasted_iota(jnp.int32, (16, G_COUNT), 1)
    for e, (elem_ref, out_ref) in enumerate(zip(elem_refs, out_refs)):
        for at, (spot, sources, k) in enumerate(parts):
            keep = (lane < cut_ref[e, spot]).astype(jnp.float32).astype(jnp.bfloat16)
            for n, source in enumerate(sources):
                ref = block_refs[source]
                rows = ref.shape[1]
                part = ref[k, :, :G_COUNT].reshape(rows // 16, 16, G_COUNT) * keep[None]
                span = pl.ds(at * TILE + n * rows, rows)
                masked[e, span, :G_COUNT] = part.reshape(rows, G_COUNT)
                masked[e, span, G_COUNT:] = ref[k, :, G_COUNT:]
        total[e] = jnp.dot(masked[e], elem_ref[:depth, :], preferred_element_type=jnp.float32)
        for at in range(len(parts)):
            out_ref[at] = total[e, pl.ds(at * TILE, TILE), :].T.astype(jnp.bfloat16)


def make_tiles(cuts, elems, chains, steps, after=()):
    depth = chains[0][0].shape[2]
    flat, parts = [], []
    for step in steps:
        sources = list(range(len(flat), len(flat) + len(chains)))
        flat += [chain[step] for chain in chains]
        for k in range(1 if step in (0, RING // 2) else 2):
            parts.append((max(0, 2 * step - 1) + k, sources, k))
    vmem = pl.BlockSpec(memory_space=pltpu.VMEM)
    free = pl.BlockSpec(memory_space=pl.ANY)
    count = len(parts)
    shape = jax.ShapeDtypeStruct((count, TILE, TILE), jnp.bfloat16)

    def kernel(*refs):
        read = 1 + len(elems) + len(flat)
        tiles_kernel(parts, len(elems), *refs[:read], *refs[read + len(after) :])

    return pl.pallas_call(
        kernel,
        out_shape=(shape,) * len(elems),
        in_specs=[pl.BlockSpec(memory_space=pltpu.SMEM)] + [vmem] * (len(elems) + len(flat)) + [free] * len(after),
        out_specs=(vmem,) * len(elems),
        scratch_shapes=[
            pltpu.VMEM((len(elems), count * TILE, depth), jnp.bfloat16),
            pltpu.VMEM((len(elems), count * TILE, TILE), jnp.float32),
        ],
        compiler_params=pltpu.CompilerParams(vmem_limit_bytes=24 << 20),
        cost_estimate=pl.CostEstimate(
            flops=2 * len(elems) * count * TILE * depth * TILE, bytes_accessed=2 * count * TILE * depth, transcendentals=0
        ),
    )(cuts, *elems, *flat, *after)


def pair_kernel(pieces, a_ref, b_ref, *refs):
    out_refs = refs[-pieces:]
    rows = out_refs[0].shape[1]
    for k, ref in enumerate(out_refs):
        ref[0] = a_ref[pl.ds(k * rows, rows), :]
        ref[1] = b_ref[pl.ds(k * rows, rows), :]


def pair(a, b, pieces, after=()):
    vmem = pl.BlockSpec(memory_space=pltpu.VMEM)
    free = pl.BlockSpec(memory_space=pl.ANY)
    shape = jax.ShapeDtypeStruct((2, a.shape[0] // pieces, a.shape[1]), a.dtype)
    return pl.pallas_call(
        functools.partial(pair_kernel, pieces),
        out_shape=(shape,) * pieces,
        in_specs=[vmem, vmem] + [free] * len(after),
        out_specs=(vmem,) * pieces,
        compiler_params=pltpu.CompilerParams(vmem_limit_bytes=8 << 20),
    )(a, b, *after)


def outbox_kernel(pos_ref, *refs):
    *in_refs, out_ref, held = refs
    at = 0
    for ref in in_refs:
        held[at : at + ref.shape[0]] = ref[...]
        at += ref.shape[0]
    held[at] = jnp.zeros(held.shape[1:], held.dtype)
    for s in range(out_ref.shape[0]):
        out_ref[s] = held[pos_ref[s]]


def make_outbox(pos, parts):
    rows, width = parts[0].shape[1:]
    slots = pos.shape[0]
    vmem = pl.BlockSpec(memory_space=pltpu.VMEM)
    return pl.pallas_call(
        outbox_kernel,
        out_shape=jax.ShapeDtypeStruct((slots, rows, width), jnp.bfloat16),
        in_specs=[pl.BlockSpec(memory_space=pltpu.SMEM)] + [vmem] * len(parts),
        out_specs=vmem,
        scratch_shapes=[pltpu.VMEM((4 * RING + 1, rows, width), jnp.bfloat16)],
        compiler_params=pltpu.CompilerParams(vmem_limit_bytes=16 << 20),
    )(pos, *parts)


def copy_kernel(x_ref, *refs):
    refs[-1][...] = x_ref[...]


def copy_after(x, after):
    vmem = pl.BlockSpec(memory_space=pltpu.VMEM)
    free = pl.BlockSpec(memory_space=pl.ANY)
    return pl.pallas_call(
        copy_kernel,
        out_shape=jax.ShapeDtypeStruct(x.shape, x.dtype),
        in_specs=[vmem] + [free] * len(after),
        out_specs=vmem,
        compiler_params=pltpu.CompilerParams(vmem_limit_bytes=8 << 20),
    )(x, *after)


def ring(held):
    blocks = [held]
    for _ in range(RING // 2 - 1):
        held = send(held, ONWARD)
        blocks.append(held)
    return blocks + [send(held[:1], ONWARD)]


def body(elem_x, elem_d, rows_x, rows_d, coulomb, screened, cutoff, owners):
    blk_len = lax.axis_size("kblk")
    me = lax.axis_index("kring")
    my_y, my_z, my_c = place(me)
    rows = jnp.concatenate([rows_x[0, 0], rows_d[0, 0]], axis=1)
    tile_rows, depth = rows.shape

    held = pair(rows, send(rows, OTHER_CORE), CHAINS)
    chains = [ring(h) for h in held]

    scaled_x = (elem_x[0, 0].astype(jnp.float32) * coulomb).astype(jnp.bfloat16)
    scaled_d = (elem_d[0, 0].astype(jnp.float32) * screened).astype(jnp.bfloat16)
    cut = cutoff[0, 0]
    cut_parts = jnp.stack([cut // 32, cut % 32]).astype(jnp.bfloat16)
    cut_parts = jnp.pad(cut_parts, ((0, 14), (0, tile_rows - cut.shape[0])))
    elem_t = jnp.concatenate([2 * scaled_x, -scaled_d], axis=1).T
    elem_t = jnp.concatenate([elem_t, cut_parts])
    far = send(elem_t, OTHER_HALF)
    far = copy_after(far, (chains[0][3],))
    far_near = send(far, OTHER_CORE)

    partner = jnp.arange(4 * RING, dtype=jnp.int32)
    p_y, p_z, p_c = place(partner)

    def in_list(core):
        ahead = jnp.where(core == 0, my_y - p_y, p_y - my_y) % RING
        off = jnp.abs(p_c - core)
        has = jnp.where((ahead == 0) | (ahead == 4), off == 0, ahead < 4)
        return has, jnp.where(ahead == 0, 0, 2 * ahead - 1 + off)

    has_mine, spot_mine = in_list(my_c)
    _, spot_other = in_list(1 - my_c)
    listed = has_mine & (p_z == my_z) & (spot_mine == jnp.arange(RING, dtype=jnp.int32)[:, None])

    def cuts_of(*elems):
        parts = jnp.stack([e[depth : depth + 2, : 4 * RING] for e in elems]).astype(jnp.int32)
        row = parts[:, 0] * 32 + parts[:, 1]
        return jnp.sum(jnp.where(listed[None], row[:, None, :], 0), axis=2)

    cuts_far, cuts_far_near = cuts_of(far), cuts_of(far_near)

    spot = jnp.where(has_mine, spot_mine, RING + spot_other) + 2 * RING * jnp.abs(p_z - my_z)
    dest = owners[0, 0, :, 0]
    same = (dest[:, None] == dest[None, :]) & (partner[None, :] < partner[:, None])
    slot_of = jnp.sum(same.astype(jnp.int32), axis=1)
    slots = jnp.arange(blk_len * CAP, dtype=jnp.int32)
    hit = slots[:, None] == (dest * CAP + slot_of)[None, :]
    pos = 4 * RING + jnp.sum(jnp.where(hit, (spot - 4 * RING)[None, :], 0), axis=1)

    steps = range(RING // 2 + 1)
    (ahead,) = make_tiles(cuts_far, (far,), chains, (0, 1, 2, 3))
    from_far = [send(ahead, OTHER_HALF)]
    (to_far_near,) = make_tiles(cuts_far_near, (far_near,), chains, steps)
    from_far_near = send(to_far_near, OTHER_BOTH)
    (to_far,) = make_tiles(cuts_far, (far,), chains, (4,), (to_far_near,))
    from_far.append(send(to_far, OTHER_HALF))
    near = send(copy_after(elem_t, (chains[1][3],)), OTHER_CORE)
    cuts_near = cuts_of(elem_t, near)
    mine, to_near = make_tiles(cuts_near, (elem_t, near), chains, steps, (to_far,))
    parts = [mine, send(to_near, OTHER_CORE)] + from_far + [from_far_near]
    outbox = make_outbox(pos, parts).reshape(blk_len, CAP, tile_rows, tile_rows)
    received = lax.all_to_all(outbox, "kblk", split_axis=0, concat_axis=0, tiled=True)
    return received[None, None]


def solution(mesh):
    in_specs = (
        P("kring", "kblk", None, None),
        P("kring", "kblk", None, None),
        P("kring", "kblk", None, None),
        P("kring", "kblk", None, None),
        P(),
        P(),
        P("kring", "kblk", None),
        P("kring", "kblk", None, None),
    )
    out_specs = P("kring", "kblk", None, None, None, None)
    return jax.shard_map(body, mesh=mesh, in_specs=in_specs, out_specs=out_specs, check_vma=False)
```

```python
import functools

import jax
import jax.numpy as jnp
from jax import lax
from jax.experimental import pallas as pl
from jax.experimental.pallas import tpu as pltpu
from jax.sharding import PartitionSpec as P

CAP = 4
RING = 8
TILE = 128
G_COUNT = 1024
CHAINS = 2


def place(i):
    return i // 4, (i // 2) % 2, i % 2


def index(y, z, c):
    return ((y % RING) * 2 + z) * 2 + c


def pairs(move):
    return [(i, index(*move(*place(i)))) for i in range(4 * RING)]


OTHER_CORE = pairs(lambda y, z, c: (y, z, 1 - c))
OTHER_HALF = pairs(lambda y, z, c: (y, 1 - z, c))
OTHER_BOTH = pairs(lambda y, z, c: (y, 1 - z, 1 - c))
ONWARD = pairs(lambda y, z, c: (y + 1 - 2 * c, z, c))


def send(x, perm):
    return lax.ppermute(x, "kring", perm)


def tiles_kernel(parts, count, cut_ref, *refs):
    elem_refs, block_refs, out_refs = refs[:count], refs[count : -count - 2], refs[-count - 2 : -2]
    masked, total = refs[-2:]
    depth = masked.shape[2]
    lane = lax.broadcasted_iota(jnp.int32, (16, G_COUNT), 1)
    for e, (elem_ref, out_ref) in enumerate(zip(elem_refs, out_refs)):
        for at, (spot, sources, k) in enumerate(parts):
            keep = (lane < cut_ref[e, spot]).astype(jnp.float32).astype(jnp.bfloat16)
            for n, source in enumerate(sources):
                ref = block_refs[source]
                rows = ref.shape[1]
                part = ref[k, :, :G_COUNT].reshape(rows // 16, 16, G_COUNT) * keep[None]
                span = pl.ds(at * TILE + n * rows, rows)
                masked[e, span, :G_COUNT] = part.reshape(rows, G_COUNT)
                masked[e, span, G_COUNT:] = ref[k, :, G_COUNT:]
        total[e] = jnp.dot(masked[e], elem_ref[:depth, :], preferred_element_type=jnp.float32)
        for at in range(len(parts)):
            out_ref[at] = total[e, pl.ds(at * TILE, TILE), :].T.astype(jnp.bfloat16)


def make_tiles(cuts, elems, chains, steps, after=()):
    depth = chains[0][0].shape[2]
    flat, parts = [], []
    for step in steps:
        sources = list(range(len(flat), len(flat) + len(chains)))
        flat += [chain[step] for chain in chains]
        for k in range(1 if step in (0, RING // 2) else 2):
            parts.append((max(0, 2 * step - 1) + k, sources, k))
    vmem = pl.BlockSpec(memory_space=pltpu.VMEM)
    free = pl.BlockSpec(memory_space=pl.ANY)
    count = len(parts)
    shape = jax.ShapeDtypeStruct((count, TILE, TILE), jnp.bfloat16)

    def kernel(*refs):
        read = 1 + len(elems) + len(flat)
        tiles_kernel(parts, len(elems), *refs[:read], *refs[read + len(after) :])

    return pl.pallas_call(
        kernel,
        out_shape=(shape,) * len(elems),
        in_specs=[pl.BlockSpec(memory_space=pltpu.SMEM)] + [vmem] * (len(elems) + len(flat)) + [free] * len(after),
        out_specs=(vmem,) * len(elems),
        scratch_shapes=[
            pltpu.VMEM((len(elems), count * TILE, depth), jnp.bfloat16),
            pltpu.VMEM((len(elems), count * TILE, TILE), jnp.float32),
        ],
        compiler_params=pltpu.CompilerParams(vmem_limit_bytes=24 << 20),
        cost_estimate=pl.CostEstimate(
            flops=2 * len(elems) * count * TILE * depth * TILE, bytes_accessed=2 * count * TILE * depth, transcendentals=0
        ),
    )(cuts, *elems, *flat, *after)


def pair_kernel(pieces, a_ref, b_ref, *refs):
    out_refs = refs[-pieces:]
    rows = out_refs[0].shape[1]
    for k, ref in enumerate(out_refs):
        ref[0] = a_ref[pl.ds(k * rows, rows), :]
        ref[1] = b_ref[pl.ds(k * rows, rows), :]


def pair(a, b, pieces, after=()):
    vmem = pl.BlockSpec(memory_space=pltpu.VMEM)
    free = pl.BlockSpec(memory_space=pl.ANY)
    shape = jax.ShapeDtypeStruct((2, a.shape[0] // pieces, a.shape[1]), a.dtype)
    return pl.pallas_call(
        functools.partial(pair_kernel, pieces),
        out_shape=(shape,) * pieces,
        in_specs=[vmem, vmem] + [free] * len(after),
        out_specs=(vmem,) * pieces,
        compiler_params=pltpu.CompilerParams(vmem_limit_bytes=8 << 20),
    )(a, b, *after)


def outbox_kernel(pos_ref, *refs):
    *in_refs, out_ref, held = refs
    at = 0
    for ref in in_refs:
        held[at : at + ref.shape[0]] = ref[...]
        at += ref.shape[0]
    held[at] = jnp.zeros(held.shape[1:], held.dtype)
    for s in range(out_ref.shape[0]):
        out_ref[s] = held[pos_ref[s]]


def make_outbox(pos, parts):
    rows, width = parts[0].shape[1:]
    slots = pos.shape[0]
    vmem = pl.BlockSpec(memory_space=pltpu.VMEM)
    return pl.pallas_call(
        outbox_kernel,
        out_shape=jax.ShapeDtypeStruct((slots, rows, width), jnp.bfloat16),
        in_specs=[pl.BlockSpec(memory_space=pltpu.SMEM)] + [vmem] * len(parts),
        out_specs=vmem,
        scratch_shapes=[pltpu.VMEM((4 * RING + 1, rows, width), jnp.bfloat16)],
        compiler_params=pltpu.CompilerParams(vmem_limit_bytes=16 << 20),
    )(pos, *parts)


def copy_kernel(x_ref, *refs):
    refs[-1][...] = x_ref[...]


def copy_after(x, after):
    vmem = pl.BlockSpec(memory_space=pltpu.VMEM)
    free = pl.BlockSpec(memory_space=pl.ANY)
    return pl.pallas_call(
        copy_kernel,
        out_shape=jax.ShapeDtypeStruct(x.shape, x.dtype),
        in_specs=[vmem] + [free] * len(after),
        out_specs=vmem,
        compiler_params=pltpu.CompilerParams(vmem_limit_bytes=8 << 20),
    )(x, *after)


def ring(held):
    blocks = [held]
    for _ in range(RING // 2 - 1):
        held = send(held, ONWARD)
        blocks.append(held)
    return blocks + [send(held[:1], ONWARD)]


def body(elem_x, elem_d, rows_x, rows_d, coulomb, screened, cutoff, owners):
    blk_len = lax.axis_size("kblk")
    me = lax.axis_index("kring")
    my_y, my_z, my_c = place(me)
    rows = jnp.concatenate([rows_x[0, 0], rows_d[0, 0]], axis=1)
    tile_rows, depth = rows.shape

    held = pair(rows, send(rows, OTHER_CORE), CHAINS)
    chains = [ring(h) for h in held]

    scaled_x = (elem_x[0, 0].astype(jnp.float32) * coulomb).astype(jnp.bfloat16)
    scaled_d = (elem_d[0, 0].astype(jnp.float32) * screened).astype(jnp.bfloat16)
    cut = cutoff[0, 0]
    cut_parts = jnp.stack([cut // 32, cut % 32]).astype(jnp.bfloat16)
    cut_parts = jnp.pad(cut_parts, ((0, 14), (0, tile_rows - cut.shape[0])))
    elem_t = jnp.concatenate([2 * scaled_x, -scaled_d], axis=1).T
    elem_t = jnp.concatenate([elem_t, cut_parts])
    far = send(elem_t, OTHER_HALF)
    far = copy_after(far, (chains[0][3],))
    far_near = send(far, OTHER_CORE)

    partner = jnp.arange(4 * RING, dtype=jnp.int32)
    p_y, p_z, p_c = place(partner)

    def in_list(core):
        ahead = jnp.where(core == 0, my_y - p_y, p_y - my_y) % RING
        off = jnp.abs(p_c - core)
        has = jnp.where((ahead == 0) | (ahead == 4), off == 0, ahead < 4)
        return has, jnp.where(ahead == 0, 0, 2 * ahead - 1 + off)

    has_mine, spot_mine = in_list(my_c)
    _, spot_other = in_list(1 - my_c)
    listed = has_mine & (p_z == my_z) & (spot_mine == jnp.arange(RING, dtype=jnp.int32)[:, None])

    def cuts_of(*elems):
        parts = jnp.stack([e[depth : depth + 2, : 4 * RING] for e in elems]).astype(jnp.int32)
        row = parts[:, 0] * 32 + parts[:, 1]
        return jnp.sum(jnp.where(listed[None], row[:, None, :], 0), axis=2)

    cuts_far, cuts_far_near = cuts_of(far), cuts_of(far_near)

    spot = jnp.where(has_mine, spot_mine, RING + spot_other) + 2 * RING * jnp.abs(p_z - my_z)
    dest = owners[0, 0, :, 0]
    same = (dest[:, None] == dest[None, :]) & (partner[None, :] < partner[:, None])
    slot_of = jnp.sum(same.astype(jnp.int32), axis=1)
    slots = jnp.arange(blk_len * CAP, dtype=jnp.int32)
    hit = slots[:, None] == (dest * CAP + slot_of)[None, :]
    pos = 4 * RING + jnp.sum(jnp.where(hit, (spot - 4 * RING)[None, :], 0), axis=1)

    steps = range(RING // 2 + 1)
    (ahead,) = make_tiles(cuts_far, (far,), chains, (0, 1, 2, 3))
    from_far = [send(ahead, OTHER_HALF)]
    (to_far_near,) = make_tiles(cuts_far_near, (far_near,), chains, steps)
    from_far_near = send(to_far_near, OTHER_BOTH)
    (to_far,) = make_tiles(cuts_far, (far,), chains, (4,), (to_far_near,))
    from_far.append(send(to_far, OTHER_HALF))
    near = send(copy_after(elem_t, (chains[1][2],)), OTHER_CORE)
    cuts_near = cuts_of(elem_t, near)
    mine, to_near = make_tiles(cuts_near, (elem_t, near), chains, steps, (to_far,))
    parts = [mine, send(to_near, OTHER_CORE)] + from_far + [from_far_near]
    outbox = make_outbox(pos, parts).reshape(blk_len, CAP, tile_rows, tile_rows)
    received = lax.all_to_all(outbox, "kblk", split_axis=0, concat_axis=0, tiled=True)
    return received[None, None]


def solution(mesh):
    in_specs = (
        P("kring", "kblk", None, None),
        P("kring", "kblk", None, None),
        P("kring", "kblk", None, None),
        P("kring", "kblk", None, None),
        P(),
        P(),
        P("kring", "kblk", None),
        P("kring", "kblk", None, None),
    )
    out_specs = P("kring", "kblk", None, None, None, None)
    return jax.shard_map(body, mesh=mesh, in_specs=in_specs, out_specs=out_specs, check_vma=False)
```

```python
import functools

import jax
import jax.numpy as jnp
from jax import lax
from jax.experimental import pallas as pl
from jax.experimental.pallas import tpu as pltpu
from jax.sharding import PartitionSpec as P

CAP = 4
RING = 8
TILE = 128
G_COUNT = 1024
CHAINS = 2


def place(i):
    return i // 4, (i // 2) % 2, i % 2


def index(y, z, c):
    return ((y % RING) * 2 + z) * 2 + c


def pairs(move):
    return [(i, index(*move(*place(i)))) for i in range(4 * RING)]


OTHER_CORE = pairs(lambda y, z, c: (y, z, 1 - c))
OTHER_HALF = pairs(lambda y, z, c: (y, 1 - z, c))
OTHER_BOTH = pairs(lambda y, z, c: (y, 1 - z, 1 - c))
ONWARD = pairs(lambda y, z, c: (y + 1 - 2 * c, z, c))


def send(x, perm):
    return lax.ppermute(x, "kring", perm)


def tiles_kernel(parts, count, cut_ref, *refs):
    elem_refs, block_refs, out_refs = refs[:count], refs[count : -count - 2], refs[-count - 2 : -2]
    masked, total = refs[-2:]
    depth = masked.shape[2]
    lane = lax.broadcasted_iota(jnp.int32, (16, G_COUNT), 1)
    for e, (elem_ref, out_ref) in enumerate(zip(elem_refs, out_refs)):
        for at, (spot, sources, k) in enumerate(parts):
            keep = (lane < cut_ref[e, spot]).astype(jnp.float32).astype(jnp.bfloat16)
            for n, source in enumerate(sources):
                ref = block_refs[source]
                rows = ref.shape[1]
                part = ref[k, :, :G_COUNT].reshape(rows // 16, 16, G_COUNT) * keep[None]
                span = pl.ds(at * TILE + n * rows, rows)
                masked[e, span, :G_COUNT] = part.reshape(rows, G_COUNT)
                masked[e, span, G_COUNT:] = ref[k, :, G_COUNT:]
        total[e] = jnp.dot(masked[e], elem_ref[:depth, :], preferred_element_type=jnp.float32)
        for at in range(len(parts)):
            out_ref[at] = total[e, pl.ds(at * TILE, TILE), :].T.astype(jnp.bfloat16)


def make_tiles(cuts, elems, chains, steps, after=()):
    depth = chains[0][0].shape[2]
    flat, parts = [], []
    for step in steps:
        sources = list(range(len(flat), len(flat) + len(chains)))
        flat += [chain[step] for chain in chains]
        for k in range(1 if step in (0, RING // 2) else 2):
            parts.append((max(0, 2 * step - 1) + k, sources, k))
    vmem = pl.BlockSpec(memory_space=pltpu.VMEM)
    free = pl.BlockSpec(memory_space=pl.ANY)
    count = len(parts)
    shape = jax.ShapeDtypeStruct((count, TILE, TILE), jnp.bfloat16)

    def kernel(*refs):
        read = 1 + len(elems) + len(flat)
        tiles_kernel(parts, len(elems), *refs[:read], *refs[read + len(after) :])

    return pl.pallas_call(
        kernel,
        out_shape=(shape,) * len(elems),
        in_specs=[pl.BlockSpec(memory_space=pltpu.SMEM)] + [vmem] * (len(elems) + len(flat)) + [free] * len(after),
        out_specs=(vmem,) * len(elems),
        scratch_shapes=[
            pltpu.VMEM((len(elems), count * TILE, depth), jnp.bfloat16),
            pltpu.VMEM((len(elems), count * TILE, TILE), jnp.float32),
        ],
        compiler_params=pltpu.CompilerParams(vmem_limit_bytes=24 << 20),
        cost_estimate=pl.CostEstimate(
            flops=16 * len(elems) * count * TILE * depth * TILE, bytes_accessed=2 * count * TILE * depth, transcendentals=0
        ),
    )(cuts, *elems, *flat, *after)


def pair_kernel(pieces, a_ref, b_ref, *refs):
    out_refs = refs[-pieces:]
    rows = out_refs[0].shape[1]
    for k, ref in enumerate(out_refs):
        ref[0] = a_ref[pl.ds(k * rows, rows), :]
        ref[1] = b_ref[pl.ds(k * rows, rows), :]


def pair(a, b, pieces, after=()):
    vmem = pl.BlockSpec(memory_space=pltpu.VMEM)
    free = pl.BlockSpec(memory_space=pl.ANY)
    shape = jax.ShapeDtypeStruct((2, a.shape[0] // pieces, a.shape[1]), a.dtype)
    return pl.pallas_call(
        functools.partial(pair_kernel, pieces),
        out_shape=(shape,) * pieces,
        in_specs=[vmem, vmem] + [free] * len(after),
        out_specs=(vmem,) * pieces,
        compiler_params=pltpu.CompilerParams(vmem_limit_bytes=8 << 20),
    )(a, b, *after)


def outbox_kernel(pos_ref, *refs):
    *in_refs, out_ref, held = refs
    at = 0
    for ref in in_refs:
        held[at : at + ref.shape[0]] = ref[...]
        at += ref.shape[0]
    held[at] = jnp.zeros(held.shape[1:], held.dtype)
    for s in range(out_ref.shape[0]):
        out_ref[s] = held[pos_ref[s]]


def make_outbox(pos, parts):
    rows, width = parts[0].shape[1:]
    slots = pos.shape[0]
    vmem = pl.BlockSpec(memory_space=pltpu.VMEM)
    return pl.pallas_call(
        outbox_kernel,
        out_shape=jax.ShapeDtypeStruct((slots, rows, width), jnp.bfloat16),
        in_specs=[pl.BlockSpec(memory_space=pltpu.SMEM)] + [vmem] * len(parts),
        out_specs=vmem,
        scratch_shapes=[pltpu.VMEM((4 * RING + 1, rows, width), jnp.bfloat16)],
        compiler_params=pltpu.CompilerParams(vmem_limit_bytes=16 << 20),
    )(pos, *parts)


def copy_kernel(x_ref, *refs):
    refs[-1][...] = x_ref[...]


def copy_after(x, after):
    vmem = pl.BlockSpec(memory_space=pltpu.VMEM)
    free = pl.BlockSpec(memory_space=pl.ANY)
    return pl.pallas_call(
        copy_kernel,
        out_shape=jax.ShapeDtypeStruct(x.shape, x.dtype),
        in_specs=[vmem] + [free] * len(after),
        out_specs=vmem,
        compiler_params=pltpu.CompilerParams(vmem_limit_bytes=8 << 20),
    )(x, *after)


def ring(held):
    blocks = [held]
    for _ in range(RING // 2 - 1):
        held = send(held, ONWARD)
        blocks.append(held)
    return blocks + [send(held[:1], ONWARD)]


def body(elem_x, elem_d, rows_x, rows_d, coulomb, screened, cutoff, owners):
    blk_len = lax.axis_size("kblk")
    me = lax.axis_index("kring")
    my_y, my_z, my_c = place(me)
    rows = jnp.concatenate([rows_x[0, 0], rows_d[0, 0]], axis=1)
    tile_rows, depth = rows.shape

    held = pair(rows, send(rows, OTHER_CORE), CHAINS)
    chains = [ring(h) for h in held]

    scaled_x = (elem_x[0, 0].astype(jnp.float32) * coulomb).astype(jnp.bfloat16)
    scaled_d = (elem_d[0, 0].astype(jnp.float32) * screened).astype(jnp.bfloat16)
    cut = cutoff[0, 0]
    cut_parts = jnp.stack([cut // 32, cut % 32]).astype(jnp.bfloat16)
    cut_parts = jnp.pad(cut_parts, ((0, 14), (0, tile_rows - cut.shape[0])))
    elem_t = jnp.concatenate([2 * scaled_x, -scaled_d], axis=1).T
    elem_t = jnp.concatenate([elem_t, cut_parts])
    far = send(elem_t, OTHER_HALF)
    far = copy_after(far, (chains[0][3],))
    far_near = send(far, OTHER_CORE)

    partner = jnp.arange(4 * RING, dtype=jnp.int32)
    p_y, p_z, p_c = place(partner)

    def in_list(core):
        ahead = jnp.where(core == 0, my_y - p_y, p_y - my_y) % RING
        off = jnp.abs(p_c - core)
        has = jnp.where((ahead == 0) | (ahead == 4), off == 0, ahead < 4)
        return has, jnp.where(ahead == 0, 0, 2 * ahead - 1 + off)

    has_mine, spot_mine = in_list(my_c)
    _, spot_other = in_list(1 - my_c)
    listed = has_mine & (p_z == my_z) & (spot_mine == jnp.arange(RING, dtype=jnp.int32)[:, None])

    def cuts_of(*elems):
        parts = jnp.stack([e[depth : depth + 2, : 4 * RING] for e in elems]).astype(jnp.int32)
        row = parts[:, 0] * 32 + parts[:, 1]
        return jnp.sum(jnp.where(listed[None], row[:, None, :], 0), axis=2)

    cuts_far, cuts_far_near = cuts_of(far), cuts_of(far_near)

    spot = jnp.where(has_mine, spot_mine, RING + spot_other) + 2 * RING * jnp.abs(p_z - my_z)
    dest = owners[0, 0, :, 0]
    same = (dest[:, None] == dest[None, :]) & (partner[None, :] < partner[:, None])
    slot_of = jnp.sum(same.astype(jnp.int32), axis=1)
    slots = jnp.arange(blk_len * CAP, dtype=jnp.int32)
    hit = slots[:, None] == (dest * CAP + slot_of)[None, :]
    pos = 4 * RING + jnp.sum(jnp.where(hit, (spot - 4 * RING)[None, :], 0), axis=1)

    steps = range(RING // 2 + 1)
    (ahead,) = make_tiles(cuts_far, (far,), chains, (0, 1, 2, 3))
    from_far = [send(ahead, OTHER_HALF)]
    (to_far_near,) = make_tiles(cuts_far_near, (far_near,), chains, steps)
    from_far_near = send(to_far_near, OTHER_BOTH)
    (to_far,) = make_tiles(cuts_far, (far,), chains, (4,), (to_far_near,))
    from_far.append(send(to_far, OTHER_HALF))
    near = send(copy_after(elem_t, (chains[1][2],)), OTHER_CORE)
    cuts_near = cuts_of(elem_t, near)
    mine, to_near = make_tiles(cuts_near, (elem_t, near), chains, steps, (to_far,))
    parts = [mine, send(to_near, OTHER_CORE)] + from_far + [from_far_near]
    outbox = make_outbox(pos, parts).reshape(blk_len, CAP, tile_rows, tile_rows)
    received = lax.all_to_all(outbox, "kblk", split_axis=0, concat_axis=0, tiled=True)
    return received[None, None]


def solution(mesh):
    in_specs = (
        P("kring", "kblk", None, None),
        P("kring", "kblk", None, None),
        P("kring", "kblk", None, None),
        P("kring", "kblk", None, None),
        P(),
        P(),
        P("kring", "kblk", None),
        P("kring", "kblk", None, None),
    )
    out_specs = P("kring", "kblk", None, None, None, None)
    return jax.shard_map(body, mesh=mesh, in_specs=in_specs, out_specs=out_specs, check_vma=False)
```
